32 devices in a mesh: seq: 4 (over z), chan: 2 (over x), batch: 4 (over y, core).
Axes of the slice: x: 2, y: 2, z: 4, core: 2. Of those that a mesh axis runs over, the one named last changes fastest.
Arguments:
- tokens: bfloat16 [131072, 1024], P(('batch', 'seq'), 'chan'), parts along dimension 0, may hold values from -6 to 6
- gate_in: bfloat16 [131072, 1024], P(('batch', 'seq'), 'chan'), parts along dimension 0, may hold values from -6 to 6
- mix_first: bfloat16 [512, 512], replicated, may hold values from -0.25 to 0.25
- mix_second: bfloat16 [64, 64], replicated, may hold values from -0.75 to 0.75
- twiddle: float32 [64, 512], P('seq'), may hold values from 0.5 to 2
- out_proj: bfloat16 [1024, 1024], replicated, may hold values from -0.1875 to 0.1875
Outputs:
- mixed: bfloat16 [131072, 1024], P(('batch', 'seq'), 'chan'), parts along dimension 0
The draws below stay inside these ranges and needn't reach their ends.
There are 4 independent parts, one for each index of `batch`. The reference program is written for one: setup_inputs(seed, part) draws one part's arguments, and reference() takes and returns one part's arrays. A program takes and returns all parts, laid end to end along the dimension named above; an argument that names none is the same for every part. Nothing has to cross between parts.
All inputs are finite; a program needn't handle non-finite values.
Results may differ from the reference program's by a relative error of at most 0.012.
Values may be sent and summed in bfloat16 or wider, within the bound.
No kernel may reach another device: no remote copies, remote signals or barrier semaphores. Data moves between devices by JAX's collectives and lax.ppermute only.
A program may use at most 128 MiB of HBM per device.

```python
import math
import jax
import jax.numpy as jnp
from jax import lax

D = 1024
B1 = 512
L = 32768
B2 = 64
N_CHAN = 2


def level_of(rng, dims, shards, low, high):
    level = 1.0
    for position, parts in shards:
        heights = jax.random.uniform(jax.random.fold_in(jax.random.fold_in(rng, 6), position), (parts,), jnp.float32, low / len(shards), high / len(shards))
        level = level * jnp.repeat(jnp.exp(heights), dims[position] // parts).reshape((-1,) + (1,) * (len(dims) - 1 - position))
    return level


def scatter_about(stream_key, extent, spread, limit, shards=(), held_as=jnp.bfloat16):
    gain = level_of(stream_key, extent, shards, -0.22, 0.18) if shards else 1.0
    result = jax.random.normal(stream_key, extent, jnp.float32) * spread * gain
    return jnp.minimum(jnp.maximum(result, -limit), limit).astype(held_as)


def setup_inputs(seed: int = 0, part: int = 0) -> dict:
    arg_keys = jax.random.split(jax.random.key(seed), 7)
    own_keys = jax.random.split(jax.random.fold_in(arg_keys[6], part), 7)
    return {
        "tokens": scatter_about(own_keys[0], (L, D), 1.0, 6.0, ((0, 4), (1, 2))),
        "gate_in": scatter_about(own_keys[1], (L, D), 1.0, 6.0, ((0, 4), (1, 2))),
        "mix_first": scatter_about(arg_keys[2], (B1, B1), B1 ** -0.5, 0.25),
        "mix_second": scatter_about(arg_keys[3], (B2, B2), B2 ** -0.5, 0.75),
        "twiddle": jnp.clip(jnp.exp(math.log(2.0) - 1.3862944 * jax.random.uniform(arg_keys[4], (B2, B1), jnp.float32) ** level_of(arg_keys[4], (B2, B1), ((0, 4),), -0.2, 0.2)), 0.5, 2.0),
        "out_proj": scatter_about(arg_keys[5], (D, D), D ** -0.5, 0.1875),
    }


def reference(tokens, gate_in, mix_first, mix_second, twiddle, out_proj):
    blocked = tokens.astype(jnp.float32).reshape(B2, B1, D)
    first_mixed = jnp.einsum('ik,bkc->bic', mix_first.astype(jnp.float32), blocked)
    first_mixed = (first_mixed * twiddle[:, :, None]).astype(jnp.bfloat16)
    second_mixed = jnp.einsum('jb,bic->jic', mix_second.astype(jnp.float32), first_mixed.astype(jnp.float32))
    second_mixed = second_mixed.astype(jnp.bfloat16)
    hidden = (second_mixed.reshape(L, D).astype(jnp.float32) * gate_in.astype(jnp.float32)).astype(jnp.bfloat16)
    group_width = D // N_CHAN

    def add_group(running, group):
        columns = lax.dynamic_slice_in_dim(hidden, group * group_width, group_width, 1)
        weight_rows = lax.dynamic_slice_in_dim(out_proj, group * group_width, group_width, 0)
        partial_term = jnp.dot(columns, weight_rows, preferred_element_type=jnp.float32).astype(jnp.bfloat16)
        partial_term = lax.optimization_barrier(partial_term)
        return running + partial_term.astype(jnp.float32), None

    total, unused = lax.scan(add_group, jnp.zeros((L, D), jnp.float32), jnp.arange(N_CHAN, dtype=jnp.int32))
    return total.astype(jnp.bfloat16)
```

```python
import functools

import jax
import jax.numpy as jnp
from jax import lax
from jax.experimental import pallas as pl
from jax.experimental.pallas import tpu as pltpu
from jax.sharding import PartitionSpec as P

ROWS = 16
VMEM = 56 * 1024 * 1024
BF16 = jnp.bfloat16
F32 = jnp.float32
ANY = pl.BlockSpec(memory_space=pl.ANY)


def call(kernel, grid, in_specs, out_specs, out_shape, scalar, args, deps=(), scratch=(), aliases=None, flops=0, nbytes=0):
    def run(scalar_ref, *refs):
        n = len(args)
        kernel(scalar_ref, refs[:n], refs[n + len(deps) :])

    return pl.pallas_call(
        run,
        grid_spec=pltpu.PrefetchScalarGridSpec(
            num_scalar_prefetch=1,
            grid=grid,
            in_specs=list(in_specs) + [ANY] * len(deps),
            out_specs=out_specs,
            scratch_shapes=list(scratch),
        ),
        out_shape=out_shape,
        input_output_aliases=aliases or {},
        compiler_params=pltpu.CompilerParams(vmem_limit_bytes=VMEM),
        cost_estimate=pl.CostEstimate(flops=flops, bytes_accessed=nbytes, transcendentals=0),
    )(scalar, *args, *deps)


def first_factor(place, tokens, weights, scale, step, size, seqs, deps):
    blocks, inner, cols = tokens.shape
    sub = size // seqs
    per = scale.shape[2]

    def kernel(place_ref, ins, outs):
        tok, wt, sc = ins
        me = place_ref[0]
        starts = [pl.multiple_of((me ^ m) * sub, sub) for m in range(seqs)]
        lhs = jnp.concatenate([wt[pl.ds(s, sub), :] for s in starts], axis=0)
        rows = jnp.concatenate([sc[0, pl.ds(s, sub), :] for s in starts], axis=0)
        for b in range(per):
            got = jnp.dot(lhs, tok[b], preferred_element_type=F32)
            got = (got * rows[:, b : b + 1]).astype(BF16)
            for m in range(seqs):
                outs[m][b] = got[m * sub : (m + 1) * sub]

    return call(
        kernel,
        (blocks // per,),
        [
            pl.BlockSpec((per, inner, cols), lambda g, p: (g, 0, 0)),
            pl.BlockSpec((size, inner), lambda g, p: (step, 0)),
            pl.BlockSpec((1, size, per), lambda g, p: (g, step, 0)),
        ],
        [pl.BlockSpec((per, sub, cols), lambda g, p: (g, 0, 0))] * seqs,
        [jax.ShapeDtypeStruct((blocks, sub, cols), BF16)] * seqs,
        place,
        (tokens, weights, scale),
        deps,
        flops=2 * blocks * size * inner * cols,
        nbytes=2 * blocks * cols * (inner + size),
    )


def second_factor(place, parts, spread, deps):
    seqs = len(parts)
    blocks, sub, cols = parts[0].shape
    height = blocks * sub
    width = min(cols, 256)

    def kernel(place_ref, ins, outs):
        sp = ins[-1]
        rhs = [ins[m][...].reshape(height, width) for m in range(seqs)]
        for o in range(seqs):
            total = None
            for m in range(seqs):
                term = jnp.dot(
                    sp[o * height : (o + 1) * height, m * height : (m + 1) * height],
                    rhs[m],
                    preferred_element_type=F32,
                )
                total = term if total is None else total + term
            outs[o][...] = total.astype(BF16).reshape(blocks, sub, width)

    spec = pl.BlockSpec((blocks, sub, width), lambda g, p: (0, 0, g))
    return call(
        kernel,
        (cols // width,),
        [spec] * seqs + [pl.BlockSpec(spread.shape, lambda g, p: (0, 0))],
        [spec] * seqs,
        [jax.ShapeDtypeStruct((blocks, sub, cols), BF16)] * seqs,
        place,
        (*parts, spread),
        deps,
        flops=2 * (seqs * height) ** 2 * cols,
        nbytes=4 * seqs * height * cols,
    )


def gate_project(place, parts, gate, proj, step, chans, deps):
    seqs = len(parts)
    blocks, sub, cols = parts[0].shape
    size = seqs * sub
    per = min(4, blocks)

    def kernel(place_ref, ins, outs):
        got, gt, ws = ins[:seqs], ins[seqs], ins[seqs + 1 :]
        outs, hidden = outs[:-1], outs[-1]
        me = place_ref[0]
        for m in range(seqs):
            rows = pl.ds(pl.multiple_of((me ^ m) * sub, sub), sub)
            hidden[:, rows, :] = (got[m][...].astype(F32) * gt[:, rows, :].astype(F32)).astype(BF16)
        lhs = hidden[...].reshape(per * size, cols)
        for q in range(chans):
            term = jnp.dot(lhs, ws[q][...], preferred_element_type=F32)
            outs[q][...] = term.astype(BF16).reshape(per, size, cols)

    out = pl.BlockSpec((per, size, cols), lambda g, p: (g, 0, 0))
    return call(
        kernel,
        (blocks // per,),
        [pl.BlockSpec((per, sub, cols), lambda g, p: (g, 0, 0))] * seqs
        + [pl.BlockSpec((per, size, cols), lambda g, p: (g, step, 0))]
        + [pl.BlockSpec((cols, cols), functools.partial(lambda q, g, p: (p[1], p[1] ^ q), q)) for q in range(chans)],
        [out] * chans,
        [jax.ShapeDtypeStruct((blocks, size, cols), BF16)] * chans,
        place,
        (*parts, gate) + (proj,) * chans,
        deps,
        scratch=[pltpu.VMEM((per, size, cols), BF16)],
        flops=2 * blocks * size * cols * cols * chans,
        nbytes=2 * blocks * size * cols * (2 + chans),
    )


def add_up(place, parts, held, shape, step, deps):
    chans = len(parts)
    blocks, size, cols = parts[0].shape
    per = min(4, blocks)

    def kernel(place_ref, ins, outs):
        total = ins[0][...].astype(F32)
        for q in range(1, chans):
            total = total + ins[q][...].astype(F32)
        outs[0][...] = total.astype(BF16)

    spec = pl.BlockSpec((per, size, cols), lambda g, p: (g, 0, 0))
    carried = () if held is None else (held,)
    return call(
        kernel,
        (blocks // per,),
        [spec] * chans,
        [pl.BlockSpec((per, size, cols), lambda g, p: (g, step, 0))],
        [jax.ShapeDtypeStruct(shape, BF16)],
        place,
        tuple(parts),
        carried + tuple(deps),
        aliases={} if held is None else {1 + chans: 0},
        flops=blocks * size * cols * chans,
        nbytes=2 * blocks * size * cols * (1 + chans),
    )[0]


def by_offset(x, axis, me, count):
    bit = 1
    while bit < count:
        shape = x.shape
        split = x.reshape(shape[:axis] + (count // (2 * bit), 2, bit) + shape[axis + 1 :])
        x = jnp.where((me & bit) != 0, jnp.flip(split, axis + 1), split).reshape(shape)
        bit *= 2
    return x


def exchange(parts, axis):
    n = len(parts)
    order = sorted(range(1, n), reverse=True)
    got = {0: parts[0]}
    for m in order:
        got[m] = lax.ppermute(parts[m], axis, [(d, d ^ m) for d in range(n)])
    return [got[m] for m in range(n)]


def body(tokens, gate_in, mix_first, mix_second, twiddle, out_proj):
    rows, cols = tokens.shape
    inner = mix_first.shape[0]
    blocks = rows // inner
    seqs, chans = lax.axis_size("seq"), lax.axis_size("chan")
    seq, chan = lax.axis_index("seq"), lax.axis_index("chan")
    steps = max(1, min(8, inner // (seqs * ROWS)))
    size = inner // steps
    sub = size // seqs
    per = min(4, blocks)
    place = jnp.stack([seq, chan]).astype(jnp.int32)
    tokens = tokens.reshape(blocks, inner, cols)
    gate = gate_in.reshape(blocks, inner, cols)
    scale = twiddle.reshape(blocks // per, per, inner).transpose(0, 2, 1)
    order = mix_second.shape[0]
    mixer = mix_second.reshape(seqs, blocks, seqs, blocks)
    mixer = by_offset(by_offset(mixer, 0, seq, seqs), 2, seq, seqs).reshape(order, order)
    spread = jnp.where(
        jnp.eye(sub, dtype=bool)[None, :, None, :], mixer[:, None, :, None], jnp.zeros((), BF16)
    ).reshape(order * sub, order * sub)

    gone, back, firsts = {}, {}, {}
    sums, out = {}, None

    def first(t, deps):
        firsts[t] = exchange(first_factor(place, tokens, mix_first, scale, t, size, seqs, deps), "seq")

    first(0, ())
    first(1, (firsts[0][0],)) if steps > 1 else None
    last = None
    for t in range(steps + 2):
        if t < steps:
            got = second_factor(place, firsts[t], spread, () if last is None else (last,))
            last = got[0]
            back[t] = exchange(got, "seq")
            if t + 2 < steps:
                first(t + 2, (last,))
                last = firsts[t + 2][0]
        if 0 <= t - 1 < steps:
            got = gate_project(place, back[t - 1], gate, out_proj, t - 1, chans, (last,))
            last = got[0]
            sums[t - 1] = exchange(got, "chan")
        if 0 <= t - 2 < steps:
            out = add_up(place, sums[t - 2], out, (blocks, inner, cols), t - 2, (last,))
            last = out if t - 2 == steps - 1 else last
    return out.reshape(rows, cols)


def solution(mesh):
    placed = (
        P(("batch", "seq"), "chan"),
        P(("batch", "seq"), "chan"),
        P(),
        P(),
        P("seq", None),
        P(),
    )
    return jax.shard_map(
        body, mesh=mesh, in_specs=placed, out_specs=P(("batch", "seq"), "chan"), check_vma=False
    )
```

```python
import functools

import jax
import jax.numpy as jnp
from jax import lax
from jax.experimental import pallas as pl
from jax.experimental.pallas import tpu as pltpu
from jax.sharding import PartitionSpec as P

ROWS = 16
PER_A = 4
PER_C = 8
PER_D = 8
WIDTH = 512
TAIL = 2
ORDER = 'ABGP'
LEAD = 2
ZORDER = (3, 2, 1)
LAG = 3
COST = 1
VMEM = 56 * 1024 * 1024
BF16 = jnp.bfloat16
F32 = jnp.float32
ANY = pl.BlockSpec(memory_space=pl.ANY)


def call(kernel, grid, in_specs, out_specs, out_shape, scalar, args, deps=(), scratch=(), aliases=None, flops=0, nbytes=0):
    def run(scalar_ref, *refs):
        n = len(args)
        kernel(scalar_ref, refs[:n], refs[n + len(deps) :])

    return pl.pallas_call(
        run,
        grid_spec=pltpu.PrefetchScalarGridSpec(
            num_scalar_prefetch=1,
            grid=grid,
            in_specs=list(in_specs) + [ANY] * len(deps),
            out_specs=out_specs,
            scratch_shapes=list(scratch),
        ),
        out_shape=out_shape,
        input_output_aliases=aliases or {},
        compiler_params=pltpu.CompilerParams(vmem_limit_bytes=VMEM),
        cost_estimate=pl.CostEstimate(flops=int(flops * COST), bytes_accessed=int(nbytes * COST), transcendentals=0),
    )(scalar, *args, *deps)


def first_factor(place, tokens, weights, twiddle, steps, size, seqs, deps):
    blocks, inner, cols = tokens.shape
    sub = size // seqs
    per = min(PER_A, blocks)
    n = len(steps)
    low = steps[0] * size

    def kernel(place_ref, ins, outs):
        tok, wt, tw = ins
        outs, lhs, turned = outs[:-2], outs[-2], outs[-1]
        me = place_ref[0]
        g = pl.program_id(0)

        @pl.when(g == 0)
        def _():
            for k in range(n):
                for m in range(seqs):
                    at = pl.ds(pl.multiple_of(low + k * size + (me ^ m) * sub, sub), sub)
                    lhs[k * size + m * sub : k * size + (m + 1) * sub, :] = wt[at, :]

        turned[...] = tw[...].T
        for k in range(n):
            rows = jnp.concatenate(
                [
                    turned[pl.ds(pl.multiple_of(low + k * size + (me ^ m) * sub, sub), sub), :]
                    for m in range(seqs)
                ],
                axis=0,
            )
            for b in range(per):
                got = jnp.dot(lhs[k * size : (k + 1) * size, :], tok[b], preferred_element_type=F32)
                got = (got * rows[:, b : b + 1]).astype(BF16)
                for m in range(seqs):
                    outs[k * seqs + m][b] = got[m * sub : (m + 1) * sub]

    return call(
        kernel,
        (blocks // per,),
        [
            pl.BlockSpec((per, inner, cols), lambda g, p: (g, 0, 0)),
            pl.BlockSpec((inner, inner), lambda g, p: (0, 0)),
            pl.BlockSpec((None, per, inner), lambda g, p: (g, 0, 0)),
        ],
        [pl.BlockSpec((per, sub, cols), lambda g, p: (g, 0, 0))] * (n * seqs),
        [jax.ShapeDtypeStruct((blocks, sub, cols), BF16)] * (n * seqs),
        place,
        (tokens, weights, twiddle.reshape(blocks // per, per, inner)),
        deps,
        scratch=[pltpu.VMEM((n * size, inner), BF16), pltpu.VMEM((inner, per), F32)],
        flops=2 * blocks * n * size * inner * cols,
        nbytes=2 * blocks * cols * (inner + n * size),
    )


def spread_out(place, mixer, blocks, sub, seqs, deps):
    order = mixer.shape[0]
    height = order * sub
    here = blocks * sub
    tall = min(height, 1024)

    def source(rows, me):
        return ((rows // here) ^ me) * blocks + (rows % here) // sub

    def kernel(place_ref, ins, outs):
        me = place_ref[0]
        base = pl.program_id(0) * tall
        down = lax.broadcasted_iota(jnp.int32, (tall, order), 0) + base
        left = (source(down, me) == lax.broadcasted_iota(jnp.int32, (tall, order), 1)).astype(BF16)
        over = lax.broadcasted_iota(jnp.int32, (order, height), 1)
        right = (source(over, me) == lax.broadcasted_iota(jnp.int32, (order, height), 0)).astype(BF16)
        some = jnp.dot(left, ins[0][...], preferred_element_type=F32).astype(BF16)
        full = jnp.dot(some, right, preferred_element_type=F32).astype(BF16)
        same = (lax.broadcasted_iota(jnp.int32, (tall, height), 0) % sub) == (
            lax.broadcasted_iota(jnp.int32, (tall, height), 1) % sub
        )
        outs[0][...] = jnp.where(same, full, jnp.zeros_like(full))

    return call(
        kernel,
        (height // tall,),
        [pl.BlockSpec((order, order), lambda g, p: (0, 0))],
        [pl.BlockSpec((tall, height), lambda g, p: (g, 0))],
        [jax.ShapeDtypeStruct((height, height), BF16)],
        place,
        (mixer,),
        deps,
        flops=2 * height * height * order,
        nbytes=2 * height * height,
    )[0]


def second_factor(place, parts, spread, cuts, deps):
    seqs = len(parts)
    blocks, sub, cols = parts[0].shape
    height = blocks * sub
    width = min(cols, WIDTH)

    def kernel(place_ref, ins, outs):
        sp = ins[-1]
        rhs = [ins[m][...].reshape(height, width) for m in range(seqs)]
        for o in range(seqs):
            total = None
            for m in range(seqs):
                term = jnp.dot(
                    sp[o * height : (o + 1) * height, m * height : (m + 1) * height],
                    rhs[m],
                    preferred_element_type=F32,
                )
                total = term if total is None else total + term
            got = total.astype(BF16).reshape(blocks, sub, width)
            for c in range(cuts):
                outs[c * seqs + o][...] = got[c * some : (c + 1) * some]

    some = blocks // cuts
    spec = pl.BlockSpec((blocks, sub, width), lambda g, p: (0, 0, g))
    out = pl.BlockSpec((some, sub, width), lambda g, p: (0, 0, g))
    return call(
        kernel,
        (cols // width,),
        [spec] * seqs + [pl.BlockSpec(spread.shape, lambda g, p: (0, 0))],
        [out] * (seqs * cuts),
        [jax.ShapeDtypeStruct((some, sub, cols), BF16)] * (seqs * cuts),
        place,
        (*parts, spread),
        deps,
        flops=2 * (seqs * height) ** 2 * cols,
        nbytes=4 * seqs * height * cols,
    )


def gate_project(place, parts, gate, proj, step, cut, chans, deps):
    seqs = len(parts)
    blocks, sub, cols = parts[0].shape
    size = seqs * sub
    per = min(PER_C, blocks)

    def kernel(place_ref, ins, outs):
        got, gt, ws = ins[:seqs], ins[seqs], ins[seqs + 1 :]
        outs, hidden = outs[:-1], outs[-1]
        me = place_ref[0]
        for m in range(seqs):
            rows = pl.ds(pl.multiple_of((me ^ m) * sub, sub), sub)
            hidden[:, rows, :] = (got[m][...].astype(F32) * gt[:, rows, :].astype(F32)).astype(BF16)
        lhs = hidden[...].reshape(per * size, cols)
        for q in range(chans):
            term = jnp.dot(lhs, ws[q][...], preferred_element_type=F32)
            outs[q][...] = term.astype(BF16).reshape(per, size, cols)

    out = pl.BlockSpec((per, size, cols), lambda g, p: (g, 0, 0))
    return call(
        kernel,
        (blocks // per,),
        [pl.BlockSpec((per, sub, cols), lambda g, p: (g, 0, 0))] * seqs
        + [pl.BlockSpec((per, size, cols), lambda g, p: (cut * (blocks // per) + g, step, 0))]
        + [pl.BlockSpec((cols, cols), functools.partial(lambda q, g, p: (p[1], p[1] ^ q), q)) for q in range(chans)],
        [out] * chans,
        [jax.ShapeDtypeStruct((blocks, size, cols), BF16)] * chans,
        place,
        (*parts, gate) + (proj,) * chans,
        deps,
        scratch=[pltpu.VMEM((per, size, cols), BF16)],
        flops=2 * blocks * size * cols * cols * chans,
        nbytes=2 * blocks * size * cols * (2 + chans),
    )


def add_up(place, parts, held, shape, step, cut, deps):
    chans = len(parts)
    blocks, size, cols = parts[0].shape
    per = min(PER_D, blocks)

    def kernel(place_ref, ins, outs):
        total = ins[0][...].astype(F32)
        for q in range(1, chans):
            total = total + ins[q][...].astype(F32)
        outs[0][...] = total.astype(BF16)

    spec = pl.BlockSpec((per, size, cols), lambda g, p: (g, 0, 0))
    carried = () if held is None else (held,)
    deps = [d for d in deps if d is not held]
    return call(
        kernel,
        (blocks // per,),
        [spec] * chans,
        [pl.BlockSpec((per, size, cols), lambda g, p: (cut * (blocks // per) + g, step, 0))],
        [jax.ShapeDtypeStruct(shape, BF16)],
        place,
        tuple(parts),
        carried + tuple(deps),
        aliases={} if held is None else {1 + chans: 0},
        flops=blocks * size * cols * chans,
        nbytes=2 * blocks * size * cols * (1 + chans),
    )[0]


def exchange(parts, axis):
    n = len(parts)
    order = [m for m in ZORDER if m < n] + [m for m in range(1, n) if m not in ZORDER]
    got = {0: parts[0]}
    for m in order:
        got[m] = lax.ppermute(parts[m], axis, [(d, d ^ m) for d in range(n)])
    return [got[m] for m in range(n)]


def body(tokens, gate_in, mix_first, mix_second, twiddle, out_proj):
    rows, cols = tokens.shape
    inner = mix_first.shape[0]
    blocks = rows // inner
    seqs, chans = lax.axis_size("seq"), lax.axis_size("chan")
    seq, chan = lax.axis_index("seq"), lax.axis_index("chan")
    steps = max(1, min(8, inner // (seqs * ROWS)))
    size = inner // steps
    sub = size // seqs
    place = jnp.stack([seq, chan]).astype(jnp.int32)
    tokens = tokens.reshape(blocks, inner, cols)
    gate = gate_in.reshape(blocks, inner, cols)
    back, firsts, sums, out = {}, {}, {}, None
    whole = (blocks, inner, cols)

    def first(t, deps):
        got = first_factor(place, tokens, mix_first, twiddle, [t], size, seqs, deps)
        firsts[t] = exchange(got, "seq")
        return got[0]

    def cuts(t):
        return TAIL if t == steps - 1 else 1

    def step_units(t):
        if t < steps - 1:
            return [(t, 0)] if t >= 0 else []
        t -= steps - 1
        return [(steps - 1, t)] if t < TAIL else []

    last = first(0, ())
    for t in range(1, min(LEAD, steps)):
        last = first(t, (last,))
    spread = spread_out(place, mix_second, blocks, sub, seqs, (last,))
    last = spread
    for t in range(steps + TAIL + LAG):
        for what in ORDER:
            if what == "B" and t < steps:
                got = second_factor(place, firsts[t], spread, cuts(t), (last,))
                last = got[0]
                for c in range(cuts(t)):
                    back[t, c] = exchange(got[c * seqs : (c + 1) * seqs], "seq")
            if what == "A" and t + LEAD < steps:
                last = first(t + LEAD, (last,))
            if what == "G":
                for u in step_units(t - 1):
                    got = gate_project(place, back[u], gate, out_proj, *u, chans, (last,))
                    last = got[0]
                    sums[u] = exchange(got, "chan")
            if what == "P":
                for u in step_units(t - LAG):
                    out = add_up(place, sums[u], out, whole, *u, (last,))
                    last = out
    return out.reshape(rows, cols)


def solution(mesh):
    placed = (
        P(("batch", "seq"), "chan"),
        P(("batch", "seq"), "chan"),
        P(),
        P(),
        P("seq", None),
        P(),
    )
    return jax.shard_map(
        body, mesh=mesh, in_specs=placed, out_specs=P(("batch", "seq"), "chan"), check_vma=False
    )
```

```python
import functools

import jax
import jax.numpy as jnp
from jax import lax
from jax.experimental import pallas as pl
from jax.experimental.pallas import tpu as pltpu
from jax.sharding import PartitionSpec as P

ROWS = 16
PER_A = 4
PER_C = 8
PER_D = 8
WIDTH = 512
TAIL = (8, 8)
ORDER = 'BGAP'
LEAD = 2
ZORDER = (3, 2, 1)
LAG = 3
COST_A = 5
COST_B = 5
COST_C = 5
COST_D = 1
COST_R = 1
DELAY = ''
ANCHOR = True
HOLD = 1
BEFORE = 1
VMEM = 56 * 1024 * 1024
BF16 = jnp.bfloat16
F32 = jnp.float32
ANY = pl.BlockSpec(memory_space=pl.ANY)


def call(kernel, grid, in_specs, out_specs, out_shape, scalar, args, deps=(), scratch=(), aliases=None, flops=0, nbytes=0):
    n, heads = len(args), 0 if scalar is None else 1

    def run(*refs):
        kernel(refs[0] if heads else None, refs[heads : heads + n], refs[heads + n + len(deps) :])

    return pl.pallas_call(
        run,
        grid_spec=pltpu.PrefetchScalarGridSpec(
            num_scalar_prefetch=heads,
            grid=grid,
            in_specs=list(in_specs) + [ANY] * len(deps),
            out_specs=out_specs,
            scratch_shapes=list(scratch),
        ),
        out_shape=out_shape,
        input_output_aliases=aliases or {},
        compiler_params=pltpu.CompilerParams(vmem_limit_bytes=VMEM),
        cost_estimate=pl.CostEstimate(flops=int(flops), bytes_accessed=int(nbytes), transcendentals=0),
    )(*([] if scalar is None else [scalar]), *args, *deps)


def fit(most, *sizes):
    return max(p for p in range(1, most + 1) if all(x % p == 0 for x in sizes))


def first_factor(tokens, weights, twiddle, steps, size, seqs, deps):
    blocks, inner, cols = tokens.shape
    sub = size // seqs
    per = min(PER_A, blocks)
    lanes = min(cols, 128)
    n = len(steps)
    low = steps[0] * size

    def kernel(place_ref, ins, outs):
        tok, wt, tw = ins
        outs, lhs, turned, scale = outs[:-3], outs[-3], outs[-2], outs[-1]
        me = lax.axis_index("seq")
        g = pl.program_id(0)

        @pl.when(g == 0)
        def _():
            turned[...] = tw[...].T
            for k in range(n):
                for m in range(seqs):
                    at = pl.ds(pl.multiple_of(low + k * size + (me ^ m) * sub, sub), sub)
                    to = slice(k * size + m * sub, k * size + (m + 1) * sub)
                    lhs[to, :] = wt[at, :]
                    column = turned[at, :]
                    for b in range(blocks):
                        scale[b, to, :] = jnp.broadcast_to(column[:, b : b + 1], (sub, lanes))

        for k in range(n):
            here = slice(k * size, (k + 1) * size)
            for b in range(per):
                got = jnp.dot(lhs[here, :], tok[b], preferred_element_type=F32)
                factor = scale[g * per + b, here, :]
                got = (got * jnp.concatenate([factor] * (cols // lanes), axis=1)).astype(BF16)
                for m in range(seqs):
                    outs[k * seqs + m][b] = got[m * sub : (m + 1) * sub]

    return call(
        kernel,
        (blocks // per,),
        [
            pl.BlockSpec((per, inner, cols), lambda g: (g, 0, 0)),
            pl.BlockSpec((inner, inner), lambda g: (0, 0)),
            pl.BlockSpec((blocks, inner), lambda g: (0, 0)),
        ],
        [pl.BlockSpec((per, sub, cols), lambda g: (g, 0, 0))] * (n * seqs),
        [jax.ShapeDtypeStruct((blocks, sub, cols), BF16)] * (n * seqs),
        None,
        (tokens, weights, twiddle),
        deps,
        scratch=[
            pltpu.VMEM((n * size, inner), BF16),
            pltpu.VMEM((inner, blocks), F32),
            pltpu.VMEM((blocks, n * size, lanes), F32),
        ],
        flops=(2 * blocks * n * size * inner * cols) * COST_A,
        nbytes=(2 * blocks * cols * (inner + n * size)) * COST_A,
    )


def released(parts, deps):
    def kernel(place_ref, ins, outs):
        pass

    return call(
        kernel,
        (1,),
        [ANY] * len(parts),
        [ANY] * len(parts),
        [jax.ShapeDtypeStruct(x.shape, x.dtype) for x in parts],
        None,
        tuple(parts),
        deps,
        aliases={k: k for k in range(len(parts))},
        flops=1000000000 * COST_R,
        nbytes=1000000 * COST_R,
    )


def spread_out(place, mixer, blocks, sub, seqs, deps):
    order = mixer.shape[0]
    height = order * sub
    here = blocks * sub
    tall = min(height, 1024)

    def source(rows, me):
        return ((rows // here) ^ me) * blocks + (rows % here) // sub

    def kernel(place_ref, ins, outs):
        me = place_ref[0]
        base = pl.program_id(0) * tall
        down = lax.broadcasted_iota(jnp.int32, (tall, order), 0) + base
        left = (source(down, me) == lax.broadcasted_iota(jnp.int32, (tall, order), 1)).astype(BF16)
        over = lax.broadcasted_iota(jnp.int32, (order, height), 1)
        right = (source(over, me) == lax.broadcasted_iota(jnp.int32, (order, height), 0)).astype(BF16)
        some = jnp.dot(left, ins[0][...], preferred_element_type=F32).astype(BF16)
        full = jnp.dot(some, right, preferred_element_type=F32).astype(BF16)
        same = (lax.broadcasted_iota(jnp.int32, (tall, height), 0) % sub) == (
            lax.broadcasted_iota(jnp.int32, (tall, height), 1) % sub
        )
        outs[0][...] = jnp.where(same, full, jnp.zeros_like(full))

    return call(
        kernel,
        (height // tall,),
        [pl.BlockSpec((order, order), lambda g, p: (0, 0))],
        [pl.BlockSpec((tall, height), lambda g, p: (g, 0))],
        [jax.ShapeDtypeStruct((height, height), BF16)],
        place,
        (mixer,),
        deps,
        flops=2 * height * height * order,
        nbytes=2 * height * height,
    )[0]


def second_factor(place, parts, spread, cuts, deps):
    seqs = len(parts)
    blocks, sub, cols = parts[0].shape
    height = blocks * sub
    width = min(cols, WIDTH)

    def kernel(place_ref, ins, outs):
        sp = ins[-1]
        rhs = [ins[m][...].reshape(height, width) for m in range(seqs)]
        for o in range(seqs):
            total = None
            for m in range(seqs):
                term = jnp.dot(
                    sp[o * height : (o + 1) * height, m * height : (m + 1) * height],
                    rhs[m],
                    preferred_element_type=F32,
                )
                total = term if total is None else total + term
            got = total.astype(BF16).reshape(blocks, sub, width)
            for c, (low, some) in enumerate(cuts):
                outs[c * seqs + o][...] = got[low : low + some]

    spec = pl.BlockSpec((blocks, sub, width), lambda g, p: (0, 0, g))
    return call(
        kernel,
        (cols // width,),
        [spec] * seqs + [pl.BlockSpec(spread.shape, lambda g, p: (0, 0))],
        [pl.BlockSpec((some, sub, width), lambda g, p: (0, 0, g)) for low, some in cuts for _ in range(seqs)],
        [jax.ShapeDtypeStruct((some, sub, cols), BF16) for low, some in cuts for _ in range(seqs)],
        place,
        (*parts, spread),
        deps,
        flops=(2 * (seqs * height) ** 2 * cols) * COST_B,
        nbytes=(4 * seqs * height * cols) * COST_B,
    )


def gate_project(place, parts, gate, proj, step, low, chans, deps):
    seqs = len(parts)
    blocks, sub, cols = parts[0].shape
    size = seqs * sub
    per = fit(PER_C, blocks, low)

    def kernel(place_ref, ins, outs):
        got, gt, ws = ins[:seqs], ins[seqs], ins[seqs + 1 :]
        outs, hidden = outs[:-1], outs[-1]
        me = place_ref[0]
        for m in range(seqs):
            rows = pl.ds(pl.multiple_of((me ^ m) * sub, sub), sub)
            hidden[:, rows, :] = (got[m][...].astype(F32) * gt[:, rows, :].astype(F32)).astype(BF16)
        lhs = hidden[...].reshape(per * size, cols)
        for q in range(chans):
            term = jnp.dot(lhs, ws[q][...], preferred_element_type=F32)
            outs[q][...] = term.astype(BF16).reshape(per, size, cols)

    out = pl.BlockSpec((per, size, cols), lambda g, p: (g, 0, 0))
    return call(
        kernel,
        (blocks // per,),
        [pl.BlockSpec((per, sub, cols), lambda g, p: (g, 0, 0))] * seqs
        + [pl.BlockSpec((per, size, cols), lambda g, p: (low // per + g, step, 0))]
        + [pl.BlockSpec((cols, cols), functools.partial(lambda q, g, p: (p[1], p[1] ^ q), q)) for q in range(chans)],
        [out] * chans,
        [jax.ShapeDtypeStruct((blocks, size, cols), BF16)] * chans,
        place,
        (*parts, gate) + (proj,) * chans,
        deps,
        scratch=[pltpu.VMEM((per, size, cols), BF16)],
        flops=(2 * blocks * size * cols * cols * chans) * COST_C,
        nbytes=(2 * blocks * size * cols * (2 + chans)) * COST_C,
    )


def add_up(place, parts, held, shape, step, low, deps):
    chans = len(parts)
    blocks, size, cols = parts[0].shape
    per = fit(PER_D, blocks, low)

    def kernel(place_ref, ins, outs):
        total = ins[0][...].astype(F32)
        for q in range(1, chans):
            total = total + ins[q][...].astype(F32)
        outs[0][...] = total.astype(BF16)

    spec = pl.BlockSpec((per, size, cols), lambda g, p: (g, 0, 0))
    carried = () if held is None else (held,)
    deps = [d for d in deps if d is not held]
    return call(
        kernel,
        (blocks // per,),
        [spec] * chans,
        [pl.BlockSpec((per, size, cols), lambda g, p: (low // per + g, step, 0))],
        [jax.ShapeDtypeStruct(shape, BF16)],
        place,
        tuple(parts),
        carried + tuple(deps),
        aliases={} if held is None else {1 + chans: 0},
        flops=(blocks * size * cols * chans) * COST_D,
        nbytes=(2 * blocks * size * cols * (1 + chans)) * COST_D,
    )[0]


def exchange(parts, axis, near=None):
    n = len(parts)
    order = [m for m in ZORDER if m < n] + [m for m in range(1, n) if m not in ZORDER]
    got = [parts[0]] + [None] * (n - 1)

    def send(m, x):
        got[m] = lax.ppermute(x, axis, [(d, d ^ m) for d in range(n)])

    for m in order:
        if m == 1 and near is not None:
            near.append(lambda deps: send(1, released([parts[1]], deps)[0]))
        else:
            send(m, parts[m])
    return got


def body(tokens, gate_in, mix_first, mix_second, twiddle, out_proj):
    rows, cols = tokens.shape
    inner = mix_first.shape[0]
    blocks = rows // inner
    seqs, chans = lax.axis_size("seq"), lax.axis_size("chan")
    seq, chan = lax.axis_index("seq"), lax.axis_index("chan")
    steps = max(1, min(8, inner // (seqs * ROWS)))
    size = inner // steps
    sub = size // seqs
    place = jnp.stack([seq, chan]).astype(jnp.int32)
    tokens = tokens.reshape(blocks, inner, cols)
    gate = gate_in.reshape(blocks, inner, cols)
    back, firsts, sums, out = {}, {}, {}, None
    whole = (blocks, inner, cols)

    def first(some, deps):
        got = first_factor(tokens, mix_first, twiddle, some, size, seqs, deps)
        return {t: got[k * seqs : (k + 1) * seqs] for k, t in enumerate(some)}

    def cuts(t):
        if t < steps - 1 or sum(TAIL) != blocks:
            return [(0, blocks)]
        return [(sum(TAIL[:c]), n) for c, n in enumerate(TAIL)]

    ends = cuts(steps - 1)

    def units(t):
        return [(t, 0)] if t >= 0 else []

    pieces = first([0], ())
    near = []

    def flush(deps):
        while near:
            near.pop(0)(deps)

    def listed(kind):
        return near if kind in DELAY else None

    firsts[0] = exchange(pieces[0], "seq", listed("0"))
    last = pieces[0][0]
    if ANCHOR and steps > 1:
        pieces.update(first(list(range(1, steps)), (last,)))
        last = pieces[1][0]
        flush((last,))
    for t in range(1, min(LEAD, steps)):
        if t not in pieces:
            pieces.update(first([t], (last,)))
            last = pieces[t][0]
            flush((last,))
        firsts[t] = exchange(pieces[t], "seq", listed("1"))
    spread = spread_out(place, mix_second, blocks, sub, seqs, (last,))
    last = spread
    flush((last,))
    def plan():
        for t in range(steps):
            for what in ORDER:
                yield what, t, units(t - 1) if what == "G" else units(t - LAG) if what == "P" else []
        over = [(t, 0) for t in range(max(0, steps - LAG), steps - 1)]
        final = [(steps - 1, low) for low, n in ends]
        for u in over[:BEFORE]:
            yield "P", steps, [u]
        yield "G", steps, final
        yield "P", steps, over[BEFORE:] + final

    for what, t, some_units in plan():
        if what == "B" and t < steps:
            got = second_factor(place, firsts[t], spread, cuts(t), (last,))
            last = got[0]
            flush((last,))
            for c, (low, n) in enumerate(cuts(t)):
                kind = "B" if t < steps - 1 else "E"
                back[t, low] = exchange(got[c * seqs : (c + 1) * seqs], "seq", listed(kind))
        if what == "A" and t + LEAD < steps:
            ahead = t + LEAD
            if ANCHOR:
                sent = released(pieces[ahead][HOLD:], (last,))
                pieces[ahead] = list(pieces[ahead][:HOLD]) + list(sent)
                last = sent[0]
            else:
                pieces.update(first([ahead], (last,)))
                last = pieces[ahead][0]
                flush((last,))
            firsts[ahead] = exchange(pieces[ahead], "seq", listed("A"))
        if what == "G":
            for u in some_units:
                if None in back[u]:
                    flush((last,))
                got = gate_project(place, back[u], gate, out_proj, *u, chans, (last,))
                last = got[0]
                flush((last,))
                sums[u] = exchange(got, "chan")
        if what == "P":
            for u in some_units:
                flush((last,))
                out = add_up(place, sums[u], out, whole, *u, (last,))
                last = out
    return out.reshape(rows, cols)


def solution(mesh):
    placed = (
        P(("batch", "seq"), "chan"),
        P(("batch", "seq"), "chan"),
        P(),
        P(),
        P("seq", None),
        P(),
    )
    return jax.shard_map(
        body, mesh=mesh, in_specs=placed, out_specs=P(("batch", "seq"), "chan"), check_vma=False
    )
```

```python
import functools

import jax
import jax.numpy as jnp
from jax import lax
from jax.experimental import pallas as pl
from jax.experimental.pallas import tpu as pltpu
from jax.sharding import PartitionSpec as P

ROWS = 16
PER_A = 4
PER_C = 8
PER_D = 8
WIDTH = 512
TAIL = (8, 8)
ORDER = 'BGAP'
LEAD = 2
ZORDER = (3, 2, 1)
LAG = 3
COST_A = 5
COST_B = 5
COST_C = 5
COST_D = 1
COST_R = 1
DELAY = ''
ANCHOR = True
HOLD = 1
BEFORE = 1
VMEM = 62 * 1024 * 1024
BF16 = jnp.bfloat16
F32 = jnp.float32
ANY = pl.BlockSpec(memory_space=pl.ANY)


def call(kernel, grid, in_specs, out_specs, out_shape, scalar, args, deps=(), scratch=(), aliases=None, flops=0, nbytes=0):
    n, heads = len(args), 0 if scalar is None else 1

    def run(*refs):
        kernel(refs[0] if heads else None, refs[heads : heads + n], refs[heads + n + len(deps) :])

    return pl.pallas_call(
        run,
        grid_spec=pltpu.PrefetchScalarGridSpec(
            num_scalar_prefetch=heads,
            grid=grid,
            in_specs=list(in_specs) + [ANY] * len(deps),
            out_specs=out_specs,
            scratch_shapes=list(scratch),
        ),
        out_shape=out_shape,
        input_output_aliases=aliases or {},
        compiler_params=pltpu.CompilerParams(vmem_limit_bytes=VMEM),
        cost_estimate=pl.CostEstimate(flops=int(flops), bytes_accessed=int(nbytes), transcendentals=0),
    )(*([] if scalar is None else [scalar]), *args, *deps)


def fit(most, *sizes):
    return max(p for p in range(1, most + 1) if all(x % p == 0 for x in sizes))


def first_factor(tokens, weights, twiddle, steps, size, seqs, deps):
    blocks, inner, cols = tokens.shape
    sub = size // seqs
    per = min(PER_A, blocks)
    lanes = min(cols, 128)
    n = len(steps)
    low = steps[0] * size

    def kernel(place_ref, ins, outs):
        tok, wt, tw = ins
        outs, lhs, turned, scale = outs[:-3], outs[-3], outs[-2], outs[-1]
        me = lax.axis_index("seq")
        g = pl.program_id(0)

        @pl.when(g == 0)
        def _():
            turned[...] = tw[...].T
            for k in range(n):
                for m in range(seqs):
                    at = pl.ds(pl.multiple_of(low + k * size + (me ^ m) * sub, sub), sub)
                    to = slice(k * size + m * sub, k * size + (m + 1) * sub)
                    lhs[to, :] = wt[at, :]
                    column = turned[at, :]
                    for b in range(blocks):
                        scale[b, to, :] = jnp.broadcast_to(column[:, b : b + 1], (sub, lanes))

        for k in range(n):
            here = slice(k * size, (k + 1) * size)
            for b in range(per):
                got = jnp.dot(lhs[here, :], tok[b], preferred_element_type=F32)
                factor = scale[g * per + b, here, :]
                got = (got * jnp.concatenate([factor] * (cols // lanes), axis=1)).astype(BF16)
                for m in range(seqs):
                    outs[k * seqs + m][b] = got[m * sub : (m + 1) * sub]

    return call(
        kernel,
        (blocks // per,),
        [
            pl.BlockSpec((per, inner, cols), lambda g: (g, 0, 0)),
            pl.BlockSpec((inner, inner), lambda g: (0, 0)),
            pl.BlockSpec((blocks, inner), lambda g: (0, 0)),
        ],
        [pl.BlockSpec((per, sub, cols), lambda g: (g, 0, 0))] * (n * seqs),
        [jax.ShapeDtypeStruct((blocks, sub, cols), BF16)] * (n * seqs),
        None,
        (tokens, weights, twiddle),
        deps,
        scratch=[
            pltpu.VMEM((n * size, inner), BF16),
            pltpu.VMEM((inner, blocks), F32),
            pltpu.VMEM((blocks, n * size, lanes), F32),
        ],
        flops=(2 * blocks * n * size * inner * cols) * COST_A,
        nbytes=(2 * blocks * cols * (inner + n * size)) * COST_A,
    )


def released(parts, deps):
    def kernel(place_ref, ins, outs):
        pass

    return call(
        kernel,
        (1,),
        [ANY] * len(parts),
        [ANY] * len(parts),
        [jax.ShapeDtypeStruct(x.shape, x.dtype) for x in parts],
        None,
        tuple(parts),
        deps,
        aliases={k: k for k in range(len(parts))},
        flops=1000000000 * COST_R,
        nbytes=1000000 * COST_R,
    )


def spread_out(place, mixer, blocks, sub, seqs, deps):
    order = mixer.shape[0]
    height = order * sub
    here = blocks * sub
    tall = min(height, 1024)

    def source(rows, me):
        return ((rows // here) ^ me) * blocks + (rows % here) // sub

    def kernel(place_ref, ins, outs):
        me = place_ref[0]
        base = pl.program_id(0) * tall
        down = lax.broadcasted_iota(jnp.int32, (tall, order), 0) + base
        left = (source(down, me) == lax.broadcasted_iota(jnp.int32, (tall, order), 1)).astype(BF16)
        over = lax.broadcasted_iota(jnp.int32, (order, height), 1)
        right = (source(over, me) == lax.broadcasted_iota(jnp.int32, (order, height), 0)).astype(BF16)
        some = jnp.dot(left, ins[0][...], preferred_element_type=F32).astype(BF16)
        full = jnp.dot(some, right, preferred_element_type=F32).astype(BF16)
        same = (lax.broadcasted_iota(jnp.int32, (tall, height), 0) % sub) == (
            lax.broadcasted_iota(jnp.int32, (tall, height), 1) % sub
        )
        outs[0][...] = jnp.where(same, full, jnp.zeros_like(full))

    return call(
        kernel,
        (height // tall,),
        [pl.BlockSpec((order, order), lambda g, p: (0, 0))],
        [pl.BlockSpec((tall, height), lambda g, p: (g, 0))],
        [jax.ShapeDtypeStruct((height, height), BF16)],
        place,
        (mixer,),
        deps,
        flops=2 * height * height * order,
        nbytes=2 * height * height,
    )[0]


def second_factor(place, parts, spread, cuts, deps):
    seqs = len(parts)
    blocks, sub, cols = parts[0].shape
    height = blocks * sub
    width = min(cols, WIDTH)

    def kernel(place_ref, ins, outs):
        sp = ins[-1]
        rhs = [ins[m][...].reshape(height, width) for m in range(seqs)]
        for o in range(seqs):
            total = None
            for m in range(seqs):
                term = jnp.dot(
                    sp[o * height : (o + 1) * height, m * height : (m + 1) * height],
                    rhs[m],
                    preferred_element_type=F32,
                )
                total = term if total is None else total + term
            got = total.astype(BF16).reshape(blocks, sub, width)
            for c, (low, some) in enumerate(cuts):
                outs[c * seqs + o][...] = got[low : low + some]

    spec = pl.BlockSpec((blocks, sub, width), lambda g, p: (0, 0, g))
    return call(
        kernel,
        (cols // width,),
        [spec] * seqs + [pl.BlockSpec(spread.shape, lambda g, p: (0, 0))],
        [pl.BlockSpec((some, sub, width), lambda g, p: (0, 0, g)) for low, some in cuts for _ in range(seqs)],
        [jax.ShapeDtypeStruct((some, sub, cols), BF16) for low, some in cuts for _ in range(seqs)],
        place,
        (*parts, spread),
        deps,
        flops=(2 * (seqs * height) ** 2 * cols) * COST_B,
        nbytes=(4 * seqs * height * cols) * COST_B,
    )


def gate_project(place, parts, gate, proj, step, low, chans, deps):
    seqs = len(parts)
    blocks, sub, cols = parts[0].shape
    size = seqs * sub
    per = fit(PER_C, blocks, low)

    def kernel(place_ref, ins, outs):
        got, gt, ws = ins[:seqs], ins[seqs], ins[seqs + 1 :]
        outs, hidden = outs[:-1], outs[-1]
        me = place_ref[0]
        for m in range(seqs):
            rows = pl.ds(pl.multiple_of((me ^ m) * sub, sub), sub)
            hidden[:, rows, :] = (got[m][...].astype(F32) * gt[:, rows, :].astype(F32)).astype(BF16)
        lhs = hidden[...].reshape(per * size, cols)
        for q in range(chans):
            term = jnp.dot(lhs, ws[q][...], preferred_element_type=F32)
            outs[q][...] = term.astype(BF16).reshape(per, size, cols)

    out = pl.BlockSpec((per, size, cols), lambda g, p: (g, 0, 0))
    return call(
        kernel,
        (blocks // per,),
        [pl.BlockSpec((per, sub, cols), lambda g, p: (g, 0, 0))] * seqs
        + [pl.BlockSpec((per, size, cols), lambda g, p: (low // per + g, step, 0))]
        + [pl.BlockSpec((cols, cols), functools.partial(lambda q, g, p: (p[1], p[1] ^ q), q)) for q in range(chans)],
        [out] * chans,
        [jax.ShapeDtypeStruct((blocks, size, cols), BF16)] * chans,
        place,
        (*parts, gate) + (proj,) * chans,
        deps,
        scratch=[pltpu.VMEM((per, size, cols), BF16)],
        flops=(2 * blocks * size * cols * cols * chans) * COST_C,
        nbytes=(2 * blocks * size * cols * (2 + chans)) * COST_C,
    )


def add_up(place, parts, held, shape, step, low, deps):
    chans = len(parts)
    blocks, size, cols = parts[0].shape
    per = fit(PER_D, blocks, low)

    def kernel(place_ref, ins, outs):
        total = ins[0][...].astype(F32)
        for q in range(1, chans):
            total = total + ins[q][...].astype(F32)
        outs[0][...] = total.astype(BF16)

    spec = pl.BlockSpec((per, size, cols), lambda g, p: (g, 0, 0))
    carried = () if held is None else (held,)
    deps = [d for d in deps if d is not held]
    return call(
        kernel,
        (blocks // per,),
        [spec] * chans,
        [pl.BlockSpec((per, size, cols), lambda g, p: (low // per + g, step, 0))],
        [jax.ShapeDtypeStruct(shape, BF16)],
        place,
        tuple(parts),
        carried + tuple(deps),
        aliases={} if held is None else {1 + chans: 0},
        flops=(blocks * size * cols * chans) * COST_D,
        nbytes=(2 * blocks * size * cols * (1 + chans)) * COST_D,
    )[0]


def exchange(parts, axis, near=None):
    n = len(parts)
    order = [m for m in ZORDER if m < n] + [m for m in range(1, n) if m not in ZORDER]
    got = [parts[0]] + [None] * (n - 1)

    def send(m, x):
        got[m] = lax.ppermute(x, axis, [(d, d ^ m) for d in range(n)])

    for m in order:
        if m == 1 and near is not None:
            near.append(lambda deps: send(1, released([parts[1]], deps)[0]))
        else:
            send(m, parts[m])
    return got


def body(tokens, gate_in, mix_first, mix_second, twiddle, out_proj):
    rows, cols = tokens.shape
    inner = mix_first.shape[0]
    blocks = rows // inner
    seqs, chans = lax.axis_size("seq"), lax.axis_size("chan")
    seq, chan = lax.axis_index("seq"), lax.axis_index("chan")
    steps = max(1, min(8, inner // (seqs * ROWS)))
    size = inner // steps
    sub = size // seqs
    place = jnp.stack([seq, chan]).astype(jnp.int32)
    tokens = tokens.reshape(blocks, inner, cols)
    gate = gate_in.reshape(blocks, inner, cols)
    back, firsts, sums, out = {}, {}, {}, None
    whole = (blocks, inner, cols)

    def first(some, deps):
        got = first_factor(tokens, mix_first, twiddle, some, size, seqs, deps)
        return {t: got[k * seqs : (k + 1) * seqs] for k, t in enumerate(some)}

    def cuts(t):
        if t < steps - 1 or sum(TAIL) != blocks:
            return [(0, blocks)]
        return [(sum(TAIL[:c]), n) for c, n in enumerate(TAIL)]

    ends = cuts(steps - 1)

    def units(t):
        return [(t, 0)] if t >= 0 else []

    pieces = first([0], ())
    near = []

    def flush(deps):
        while near:
            near.pop(0)(deps)

    def listed(kind):
        return near if kind in DELAY else None

    firsts[0] = exchange(pieces[0], "seq", listed("0"))
    last = pieces[0][0]
    if ANCHOR and steps > 1:
        pieces.update(first(list(range(1, steps)), (last,)))
        last = pieces[1][0]
        flush((last,))
    for t in range(1, min(LEAD, steps)):
        if t not in pieces:
            pieces.update(first([t], (last,)))
            last = pieces[t][0]
            flush((last,))
        firsts[t] = exchange(pieces[t], "seq", listed("1"))
    spread = spread_out(place, mix_second, blocks, sub, seqs, (last,))
    last = spread
    flush((last,))
    def plan():
        for t in range(steps):
            for what in ORDER:
                yield what, t, units(t - 1) if what == "G" else units(t - LAG) if what == "P" else []
        over = [(t, 0) for t in range(max(0, steps - LAG), steps - 1)]
        final = [(steps - 1, low) for low, n in ends]
        for u in over[:BEFORE]:
            yield "P", steps, [u]
        yield "G", steps, final
        yield "P", steps, over[BEFORE:] + final

    for what, t, some_units in plan():
        if what == "B" and t < steps:
            got = second_factor(place, firsts[t], spread, cuts(t), (last,))
            last = got[0]
            flush((last,))
            for c, (low, n) in enumerate(cuts(t)):
                kind = "B" if t < steps - 1 else "E"
                back[t, low] = exchange(got[c * seqs : (c + 1) * seqs], "seq", listed(kind))
        if what == "A" and t + LEAD < steps:
            ahead = t + LEAD
            if ANCHOR:
                sent = released(pieces[ahead][HOLD:], (last,))
                pieces[ahead] = list(pieces[ahead][:HOLD]) + list(sent)
                last = sent[0]
            else:
                pieces.update(first([ahead], (last,)))
                last = pieces[ahead][0]
                flush((last,))
            firsts[ahead] = exchange(pieces[ahead], "seq", listed("A"))
        if what == "G":
            for u in some_units:
                if None in back[u]:
                    flush((last,))
                got = gate_project(place, back[u], gate, out_proj, *u, chans, (last,))
                last = got[0]
                flush((last,))
                sums[u] = exchange(got, "chan")
        if what == "P":
            for u in some_units:
                flush((last,))
                out = add_up(place, sums[u], out, whole, *u, (last,))
                last = out
    return out.reshape(rows, cols)


def solution(mesh):
    placed = (
        P(("batch", "seq"), "chan"),
        P(("batch", "seq"), "chan"),
        P(),
        P(),
        P("seq", None),
        P(),
    )
    return jax.shard_map(
        body, mesh=mesh, in_specs=placed, out_specs=P(("batch", "seq"), "chan"), check_vma=False
    )
```

```python
import functools

import jax
import jax.numpy as jnp
from jax import lax
from jax.experimental import pallas as pl
from jax.experimental.pallas import tpu as pltpu
from jax.sharding import PartitionSpec as P

ROWS = 16
PER_A = 4
PER_C = 8
PER_D = 8
WIDTH = 512
TAIL = (8, 8)
ORDER = 'BGAP'
LEAD = 2
ZORDER = (3, 2, 1)
LAG = 3
COST_A = 1
COST_B = 5
COST_C = 5
COST_D = 1
COST_R = 1
DELAY = ''
ANCHOR = True
HOLD = 1
BEFORE = 1
VMEM = 64 * 1024 * 1024
BF16 = jnp.bfloat16
F32 = jnp.float32
ANY = pl.BlockSpec(memory_space=pl.ANY)


def call(kernel, grid, in_specs, out_specs, out_shape, scalar, args, deps=(), scratch=(), aliases=None, flops=0, nbytes=0):
    n, heads = len(args), 0 if scalar is None else 1

    def run(*refs):
        kernel(refs[0] if heads else None, refs[heads : heads + n], refs[heads + n + len(deps) :])

    return pl.pallas_call(
        run,
        grid_spec=pltpu.PrefetchScalarGridSpec(
            num_scalar_prefetch=heads,
            grid=grid,
            in_specs=list(in_specs) + [ANY] * len(deps),
            out_specs=out_specs,
            scratch_shapes=list(scratch),
        ),
        out_shape=out_shape,
        input_output_aliases=aliases or {},
        compiler_params=pltpu.CompilerParams(vmem_limit_bytes=VMEM),
        cost_estimate=pl.CostEstimate(flops=int(flops), bytes_accessed=int(nbytes), transcendentals=0),
    )(*([] if scalar is None else [scalar]), *args, *deps)


def fit(most, *sizes):
    return max(p for p in range(1, most + 1) if all(x % p == 0 for x in sizes))


def first_factor(tokens, weights, twiddle, steps, size, seqs, deps):
    blocks, inner, cols = tokens.shape
    sub = size // seqs
    per = min(PER_A, blocks)
    lanes = min(cols, 128)
    n = len(steps)
    low = steps[0] * size

    def kernel(place_ref, ins, outs):
        tok, wt, tw = ins
        outs, lhs, turned, scale = outs[:-3], outs[-3], outs[-2], outs[-1]
        me = lax.axis_index("seq")
        g = pl.program_id(0)

        @pl.when(g == 0)
        def _():
            turned[...] = tw[...].T
            for k in range(n):
                for m in range(seqs):
                    at = pl.ds(pl.multiple_of(low + k * size + (me ^ m) * sub, sub), sub)
                    to = slice(k * size + m * sub, k * size + (m + 1) * sub)
                    lhs[to, :] = wt[at, :]
                    column = turned[at, :]
                    for b in range(blocks):
                        scale[b, to, :] = jnp.broadcast_to(column[:, b : b + 1], (sub, lanes))

        for k in range(n):
            here = slice(k * size, (k + 1) * size)
            for b in range(per):
                got = jnp.dot(lhs[here, :], tok[b], preferred_element_type=F32)
                factor = scale[g * per + b, here, :]
                got = (got * jnp.concatenate([factor] * (cols // lanes), axis=1)).astype(BF16)
                for m in range(seqs):
                    outs[k * seqs + m][b] = got[m * sub : (m + 1) * sub]

    return call(
        kernel,
        (blocks // per,),
        [
            pl.BlockSpec((per, inner, cols), lambda g: (g, 0, 0)),
            pl.BlockSpec((inner, inner), lambda g: (0, 0)),
            pl.BlockSpec((blocks, inner), lambda g: (0, 0)),
        ],
        [pl.BlockSpec((per, sub, cols), lambda g: (g, 0, 0))] * (n * seqs),
        [jax.ShapeDtypeStruct((blocks, sub, cols), BF16)] * (n * seqs),
        None,
        (tokens, weights, twiddle),
        deps,
        scratch=[
            pltpu.VMEM((n * size, inner), BF16),
            pltpu.VMEM((inner, blocks), F32),
            pltpu.VMEM((blocks, n * size, lanes), F32),
        ],
        flops=(2 * blocks * n * size * inner * cols) * COST_A,
        nbytes=(2 * blocks * cols * (inner + n * size)) * COST_A,
    )


def released(parts, deps):
    def kernel(place_ref, ins, outs):
        pass

    return call(
        kernel,
        (1,),
        [ANY] * len(parts),
        [ANY] * len(parts),
        [jax.ShapeDtypeStruct(x.shape, x.dtype) for x in parts],
        None,
        tuple(parts),
        deps,
        aliases={k: k for k in range(len(parts))},
        flops=1000000000 * COST_R,
        nbytes=1000000 * COST_R,
    )


def spread_out(place, mixer, blocks, sub, seqs, deps):
    order = mixer.shape[0]
    height = order * sub
    here = blocks * sub
    tall = min(height, 1024)

    def source(rows, me):
        return ((rows // here) ^ me) * blocks + (rows % here) // sub

    def kernel(place_ref, ins, outs):
        me = place_ref[0]
        base = pl.program_id(0) * tall
        down = lax.broadcasted_iota(jnp.int32, (tall, order), 0) + base
        left = (source(down, me) == lax.broadcasted_iota(jnp.int32, (tall, order), 1)).astype(BF16)
        over = lax.broadcasted_iota(jnp.int32, (order, height), 1)
        right = (source(over, me) == lax.broadcasted_iota(jnp.int32, (order, height), 0)).astype(BF16)
        some = jnp.dot(left, ins[0][...], preferred_element_type=F32).astype(BF16)
        full = jnp.dot(some, right, preferred_element_type=F32).astype(BF16)
        same = (lax.broadcasted_iota(jnp.int32, (tall, height), 0) % sub) == (
            lax.broadcasted_iota(jnp.int32, (tall, height), 1) % sub
        )
        outs[0][...] = jnp.where(same, full, jnp.zeros_like(full))

    return call(
        kernel,
        (height // tall,),
        [pl.BlockSpec((order, order), lambda g, p: (0, 0))],
        [pl.BlockSpec((tall, height), lambda g, p: (g, 0))],
        [jax.ShapeDtypeStruct((height, height), BF16)],
        place,
        (mixer,),
        deps,
        flops=2 * height * height * order,
        nbytes=2 * height * height,
    )[0]


def second_factor(place, parts, spread, cuts, deps):
    seqs = len(parts)
    blocks, sub, cols = parts[0].shape
    height = blocks * sub
    width = min(cols, WIDTH)

    def kernel(place_ref, ins, outs):
        sp = ins[-1]
        rhs = [ins[m][...].reshape(height, width) for m in range(seqs)]
        for o in range(seqs):
            total = None
            for m in range(seqs):
                term = jnp.dot(
                    sp[o * height : (o + 1) * height, m * height : (m + 1) * height],
                    rhs[m],
                    preferred_element_type=F32,
                )
                total = term if total is None else total + term
            got = total.astype(BF16).reshape(blocks, sub, width)
            for c, (low, some) in enumerate(cuts):
                outs[c * seqs + o][...] = got[low : low + some]

    spec = pl.BlockSpec((blocks, sub, width), lambda g, p: (0, 0, g))
    return call(
        kernel,
        (cols // width,),
        [spec] * seqs + [pl.BlockSpec(spread.shape, lambda g, p: (0, 0))],
        [pl.BlockSpec((some, sub, width), lambda g, p: (0, 0, g)) for low, some in cuts for _ in range(seqs)],
        [jax.ShapeDtypeStruct((some, sub, cols), BF16) for low, some in cuts for _ in range(seqs)],
        place,
        (*parts, spread),
        deps,
        flops=(2 * (seqs * height) ** 2 * cols) * COST_B,
        nbytes=(4 * seqs * height * cols) * COST_B,
    )


def gate_project(place, parts, gate, proj, step, low, chans, deps):
    seqs = len(parts)
    blocks, sub, cols = parts[0].shape
    size = seqs * sub
    per = fit(PER_C, blocks, low)

    def kernel(place_ref, ins, outs):
        got, gt, ws = ins[:seqs], ins[seqs], ins[seqs + 1 :]
        outs, hidden = outs[:-1], outs[-1]
        me = place_ref[0]
        for m in range(seqs):
            rows = pl.ds(pl.multiple_of((me ^ m) * sub, sub), sub)
            hidden[:, rows, :] = (got[m][...].astype(F32) * gt[:, rows, :].astype(F32)).astype(BF16)
        lhs = hidden[...].reshape(per * size, cols)
        for q in range(chans):
            term = jnp.dot(lhs, ws[q][...], preferred_element_type=F32)
            outs[q][...] = term.astype(BF16).reshape(per, size, cols)

    out = pl.BlockSpec((per, size, cols), lambda g, p: (g, 0, 0))
    return call(
        kernel,
        (blocks // per,),
        [pl.BlockSpec((per, sub, cols), lambda g, p: (g, 0, 0))] * seqs
        + [pl.BlockSpec((per, size, cols), lambda g, p: (low // per + g, step, 0))]
        + [pl.BlockSpec((cols, cols), functools.partial(lambda q, g, p: (p[1], p[1] ^ q), q)) for q in range(chans)],
        [out] * chans,
        [jax.ShapeDtypeStruct((blocks, size, cols), BF16)] * chans,
        place,
        (*parts, gate) + (proj,) * chans,
        deps,
        scratch=[pltpu.VMEM((per, size, cols), BF16)],
        flops=(2 * blocks * size * cols * cols * chans) * COST_C,
        nbytes=(2 * blocks * size * cols * (2 + chans)) * COST_C,
    )


def add_up(place, parts, held, shape, step, low, deps):
    chans = len(parts)
    blocks, size, cols = parts[0].shape
    per = fit(PER_D, blocks, low)

    def kernel(place_ref, ins, outs):
        total = ins[0][...].astype(F32)
        for q in range(1, chans):
            total = total + ins[q][...].astype(F32)
        outs[0][...] = total.astype(BF16)

    spec = pl.BlockSpec((per, size, cols), lambda g, p: (g, 0, 0))
    carried = () if held is None else (held,)
    deps = [d for d in deps if d is not held]
    return call(
        kernel,
        (blocks // per,),
        [spec] * chans,
        [pl.BlockSpec((per, size, cols), lambda g, p: (low // per + g, step, 0))],
        [jax.ShapeDtypeStruct(shape, BF16)],
        place,
        tuple(parts),
        carried + tuple(deps),
        aliases={} if held is None else {1 + chans: 0},
        flops=(blocks * size * cols * chans) * COST_D,
        nbytes=(2 * blocks * size * cols * (1 + chans)) * COST_D,
    )[0]


def exchange(parts, axis, near=None):
    n = len(parts)
    order = [m for m in ZORDER if m < n] + [m for m in range(1, n) if m not in ZORDER]
    got = [parts[0]] + [None] * (n - 1)

    def send(m, x):
        got[m] = lax.ppermute(x, axis, [(d, d ^ m) for d in range(n)])

    for m in order:
        if m == 1 and near is not None:
            near.append(lambda deps: send(1, released([parts[1]], deps)[0]))
        else:
            send(m, parts[m])
    return got


def body(tokens, gate_in, mix_first, mix_second, twiddle, out_proj):
    rows, cols = tokens.shape
    inner = mix_first.shape[0]
    blocks = rows // inner
    seqs, chans = lax.axis_size("seq"), lax.axis_size("chan")
    seq, chan = lax.axis_index("seq"), lax.axis_index("chan")
    steps = max(1, min(8, inner // (seqs * ROWS)))
    size = inner // steps
    sub = size // seqs
    place = jnp.stack([seq, chan]).astype(jnp.int32)
    tokens = tokens.reshape(blocks, inner, cols)
    gate = gate_in.reshape(blocks, inner, cols)
    back, firsts, sums, out = {}, {}, {}, None
    whole = (blocks, inner, cols)

    def first(some, deps):
        got = first_factor(tokens, mix_first, twiddle, some, size, seqs, deps)
        return {t: got[k * seqs : (k + 1) * seqs] for k, t in enumerate(some)}

    def cuts(t):
        if t < steps - 1 or sum(TAIL) != blocks:
            return [(0, blocks)]
        return [(sum(TAIL[:c]), n) for c, n in enumerate(TAIL)]

    ends = cuts(steps - 1)

    def units(t):
        return [(t, 0)] if t >= 0 else []

    pieces = first([0], ())
    near = []

    def flush(deps):
        while near:
            near.pop(0)(deps)

    def listed(kind):
        return near if kind in DELAY else None

    firsts[0] = exchange(pieces[0], "seq", listed("0"))
    last = pieces[0][0]
    if ANCHOR and steps > 1:
        pieces.update(first(list(range(1, steps)), (last,)))
        last = pieces[1][0]
        flush((last,))
    for t in range(1, min(LEAD, steps)):
        if t not in pieces:
            pieces.update(first([t], (last,)))
            last = pieces[t][0]
            flush((last,))
        firsts[t] = exchange(pieces[t], "seq", listed("1"))
    spread = spread_out(place, mix_second, blocks, sub, seqs, (last,))
    last = spread
    flush((last,))
    def plan():
        for t in range(steps):
            for what in ORDER:
                yield what, t, units(t - 1) if what == "G" else units(t - LAG) if what == "P" else []
        over = [(t, 0) for t in range(max(0, steps - LAG), steps - 1)]
        final = [(steps - 1, low) for low, n in ends]
        for u in over[:BEFORE]:
            yield "P", steps, [u]
        yield "G", steps, final
        yield "P", steps, over[BEFORE:] + final

    for what, t, some_units in plan():
        if what == "B" and t < steps:
            got = second_factor(place, firsts[t], spread, cuts(t), (last,))
            last = got[0]
            flush((last,))
            for c, (low, n) in enumerate(cuts(t)):
                kind = "B" if t < steps - 1 else "E"
                back[t, low] = exchange(got[c * seqs : (c + 1) * seqs], "seq", listed(kind))
        if what == "A" and t + LEAD < steps:
            ahead = t + LEAD
            if ANCHOR:
                sent = released(pieces[ahead][HOLD:], (last,))
                pieces[ahead] = list(pieces[ahead][:HOLD]) + list(sent)
                last = sent[0]
            else:
                pieces.update(first([ahead], (last,)))
                last = pieces[ahead][0]
                flush((last,))
            firsts[ahead] = exchange(pieces[ahead], "seq", listed("A"))
        if what == "G":
            for u in some_units:
                if None in back[u]:
                    flush((last,))
                got = gate_project(place, back[u], gate, out_proj, *u, chans, (last,))
                last = got[0]
                flush((last,))
                sums[u] = exchange(got, "chan")
        if what == "P":
            for u in some_units:
                flush((last,))
                out = add_up(place, sums[u], out, whole, *u, (last,))
                last = out
    return out.reshape(rows, cols)


def solution(mesh):
    placed = (
        P(("batch", "seq"), "chan"),
        P(("batch", "seq"), "chan"),
        P(),
        P(),
        P("seq", None),
        P(),
    )
    return jax.shard_map(
        body, mesh=mesh, in_specs=placed, out_specs=P(("batch", "seq"), "chan"), check_vma=False
    )
```
